256 devices in a mesh: space: 32 (over y_hi, z, core), panel: 8 (over y_lo, x).
Axes of the slice: x: 4, y: 4 (y_hi: 2, y_lo: 2; y = y_hi * 2 + y_lo), z: 8, core: 2. Of those that a mesh axis runs over, the one named last changes fastest.
Arguments:
- fields: float32 [98304, 256], P(('space', 'panel')), may hold values from -6 to 6
- inverse_blocks: bfloat16 [98304, 4096], P(('space', 'panel'))
- kernel_blocks: bfloat16 [98304, 4096], P(('space', 'panel'))
- block_pattern: int32 [32, 24, 32], P('space', 'panel'), may hold values 0 or 1
- margin_rows: int32 [32, 2, 512], P('space'), may hold values from 0 to 3071, as said below
- coarse_basis: bfloat16 [98304, 256], P(('space', 'panel')), may hold values from -0.109375 to 0.109375
- coarse_inverse: bfloat16 [8192, 8192], P('space', 'panel')
Outputs:
- solution: float32 [98304, 256], P(('space', 'panel'))
- residual: float32 [98304, 256], P(('space', 'panel'))
The draws below stay inside these ranges and needn't reach their ends.
Inputs may be any that keep to these rules, and one draw needn't show every extreme that they name: `margin_rows`: within one subdomain and one side the 512 row numbers are distinct.
All inputs are finite; a program needn't handle non-finite values. No bound on the sum of `block_pattern` on one device may be relied on, other than what follows from the above.
Results may differ from the reference program's by a relative error of at most 0.011.
Values may be sent and summed in bfloat16 or wider, within the bound.
No kernel may reach another device: no remote copies, remote signals or barrier semaphores. Data moves between devices by JAX's collectives and lax.ppermute only.
A program may use at most 64 MiB of HBM per device.

```python
import jax
import jax.numpy as jnp
from jax import lax

OWN = 3072
OVL = 1024
SUB = 4096
TILE = 128
LAND_SUB = 256
NRHS = 256
SUBDOMAINS = 32
POINTS = 98304
LANDMARKS = 8192
LAND_PANEL = 32
N_PANEL = 8


def rough_part(key, shape):
    return jax.random.normal(key, shape, jnp.float32)


def draw_inverse_blocks(key, part):
    key = jax.random.fold_in(key, 11)
    first_key, second_key = jax.random.split(key)
    row_index = lax.broadcasted_iota(jnp.int32, (POINTS, SUB), 0) % OWN
    col_index = lax.broadcasted_iota(jnp.int32, (POINTS, SUB), 1)
    diagonal = jax.random.uniform(second_key, (POINTS, 1), jnp.float32, 0.5, 1.5)
    off_part = rough_part(first_key, (POINTS, SUB)) * (0.7 / SUB ** 0.5)
    return (off_part + jnp.where(row_index == col_index, diagonal, 0.0)).astype(jnp.bfloat16)


def draw_kernel_blocks(key, part):
    key = jax.random.fold_in(key, 12)
    first_key, second_key = jax.random.split(key)
    row_index = lax.broadcasted_iota(jnp.int32, (POINTS, SUB), 0) % OWN
    col_index = lax.broadcasted_iota(jnp.int32, (POINTS, SUB), 1)
    diagonal = jax.random.uniform(second_key, (POINTS, 1), jnp.float32, 0.8, 1.2)
    off_part = rough_part(first_key, (POINTS, SUB)) * (0.5 / SUB ** 0.5)
    return (off_part + jnp.where(row_index == col_index, diagonal, 0.0)).astype(jnp.bfloat16)


def draw_coarse_inverse(key, part):
    key = jax.random.fold_in(key, 13)
    first_key, second_key = jax.random.split(key)
    row_index = lax.broadcasted_iota(jnp.int32, (LANDMARKS, LANDMARKS), 0)
    col_index = lax.broadcasted_iota(jnp.int32, (LANDMARKS, LANDMARKS), 1)
    owner = row_index // LAND_SUB
    within = row_index % LAND_SUB
    column_of = within // LAND_PANEL * (SUBDOMAINS * LAND_PANEL) + owner * LAND_PANEL + within % LAND_PANEL
    diagonal = jax.random.uniform(second_key, (LANDMARKS, 1), jnp.float32, 0.5, 1.5)
    off_part = rough_part(first_key, (LANDMARKS, LANDMARKS)) * (0.6 / LANDMARKS ** 0.5)
    return (off_part + jnp.where(column_of == col_index, diagonal, 0.0)).astype(jnp.bfloat16)


def draw_margin_rows(key, part):
    key = jax.random.fold_in(key, 14)
    keys = jax.random.split(key, SUBDOMAINS * 2)

    def one_list(single):
        return jax.random.permutation(single, OWN)[:OVL // 2].astype(jnp.int32)
    return jax.vmap(one_list)(keys).reshape(SUBDOMAINS, 2, OVL // 2)


def place_ends(drawn, own_key, low, largest):
    place = [jax.random.randint(jax.random.fold_in(own_key, axis), (), 0, length) for axis, length in enumerate(drawn.shape)]
    longest = drawn.shape.index(max(drawn.shape))
    beside = place[:longest] + [(place[longest] + 1) % drawn.shape[longest]] + place[longest + 1:]
    return drawn.at[tuple(place)].set(low).at[tuple(beside)].set(largest)


def block_scale(key, dims, cuts, least, high):
    gain, own = 1.0, jax.random.fold_in(key, 6)
    for dim, shards_of in cuts:
        draws = jnp.exp(jax.random.uniform(jax.random.fold_in(own, dim), (shards_of,), jnp.float32, least / len(cuts), high / len(cuts)))
        gain = gain * jnp.repeat(draws, dims[dim] // shards_of).reshape([-1 if axis == dim else 1 for axis in range(len(dims))])
    return gain


def scatter_about(key, shape, deviation, bound, cuts=(), kind=jnp.bfloat16):
    result = deviation * jax.random.normal(key, shape, jnp.float32)
    if cuts:
        result = result * block_scale(key, shape, cuts, -0.22, 0.18)
    return jnp.clip(result, -bound, bound).astype(kind)


def setup_inputs(seed: int = 0) -> dict:
    key_list = jax.random.split(jax.random.key(seed), 8)
    fields = scatter_about(key_list[0], (POINTS, NRHS), 1.0, 6.0, ((0, 256),), jnp.float32)
    inverse_blocks = draw_inverse_blocks(jax.random.fold_in(key_list[7], 71), 0)
    kernel_blocks = draw_kernel_blocks(jax.random.fold_in(key_list[7], 71), 0)
    block_pattern = place_ends((jax.random.randint(key_list[3], (SUBDOMAINS, OWN // TILE, SUB // TILE), 0, 4) < 3).astype(jnp.int32), jax.random.fold_in(key_list[3], 1), 0, 1)
    margin_rows = draw_margin_rows(jax.random.fold_in(key_list[7], 71), 0)
    coarse_basis = scatter_about(key_list[5], (POINTS, LAND_SUB), OWN ** -0.5, 0.109375, ((0, 256),))
    coarse_inverse = draw_coarse_inverse(jax.random.fold_in(key_list[7], 71), 0)
    return dict(fields=fields, inverse_blocks=inverse_blocks, kernel_blocks=kernel_blocks, block_pattern=block_pattern, margin_rows=margin_rows, coarse_basis=coarse_basis, coarse_inverse=coarse_inverse)


def extend(values, margin_rows):
    owned = values.reshape(SUBDOMAINS, OWN, NRHS)
    nothing = jnp.zeros((1, OWN, NRHS), values.dtype)
    prior_blocks = jnp.concatenate([nothing, owned[:-1]], 0)
    later_blocks = jnp.concatenate([owned[1:], nothing], 0)
    from_left = jnp.take_along_axis(prior_blocks, margin_rows[:, 0, :, None].astype(jnp.int32), axis=1)
    from_right = jnp.take_along_axis(later_blocks, margin_rows[:, 1, :, None].astype(jnp.int32), axis=1)
    return jnp.concatenate([owned, from_left, from_right], 1)


def blockwise(matrices, extended):
    def one_block(couple):
        return jnp.dot(couple[0], couple[1], preferred_element_type=jnp.float32)
    return lax.map(one_block, (matrices, extended)).reshape(POINTS, NRHS)


def kernel_apply(values, kernel_blocks, block_pattern, margin_rows):
    extended = extend(values, margin_rows)
    kernels = kernel_blocks.reshape(SUBDOMAINS, OWN // TILE, TILE, SUB // TILE, TILE)

    def one_block(triple):
        masked = triple[0] * triple[1].astype(jnp.bfloat16)[:, None, :, None]
        return jnp.dot(masked.reshape(OWN, SUB), triple[2], preferred_element_type=jnp.float32)
    return lax.map(one_block, (kernels, block_pattern, extended)).reshape(POINTS, NRHS)


def precondition(resid, inverse_blocks, margin_rows, coarse_basis, coarse_inverse):
    rounded = resid.astype(jnp.bfloat16)
    extended = extend(rounded, margin_rows)
    local = blockwise(inverse_blocks.reshape(SUBDOMAINS, OWN, SUB), extended)
    basis = coarse_basis.reshape(SUBDOMAINS, OWN, LAND_SUB)
    owned = rounded.reshape(SUBDOMAINS, OWN, NRHS)

    def project(couple):
        return lax.dot_general(couple[0], couple[1], (((0,), (0,)), ((), ())), preferred_element_type=jnp.float32)
    coarse_rhs = lax.map(project, (basis, owned))
    coarse_rounded = coarse_rhs.astype(jnp.bfloat16)
    ordered = coarse_rounded.reshape(SUBDOMAINS, N_PANEL, LAND_PANEL, NRHS).transpose(1, 0, 2, 3).reshape(LANDMARKS, NRHS)
    coarse_values = jnp.dot(coarse_inverse, ordered, preferred_element_type=jnp.float32)
    values_rounded = coarse_values.astype(jnp.bfloat16).reshape(SUBDOMAINS, LAND_SUB, NRHS)
    coarse_part = blockwise(basis, values_rounded)
    return local + coarse_part


def reference(fields, inverse_blocks, kernel_blocks, block_pattern, margin_rows, coarse_basis, coarse_inverse):
    first = precondition(fields, inverse_blocks, margin_rows, coarse_basis, coarse_inverse)
    middle = fields - kernel_apply(first.astype(jnp.bfloat16), kernel_blocks, block_pattern, margin_rows)
    solution = first + precondition(middle, inverse_blocks, margin_rows, coarse_basis, coarse_inverse)
    residual = fields - kernel_apply(solution.astype(jnp.bfloat16), kernel_blocks, block_pattern, margin_rows)
    return solution, residual
```

```python
import functools

import jax
import jax.numpy as jnp
from jax import lax
from jax.experimental import pallas as pl
from jax.experimental.pallas import tpu as pltpu
from jax.sharding import PartitionSpec as P

BF = jnp.bfloat16
F32 = jnp.float32
N_Y, N_X, N_CORE = 2, 4, 2
ORDER = (0, 1, 3, 2)
VMEM_LIMIT = 14 * 2**20


def params():
    return pltpu.CompilerParams(vmem_limit_bytes=VMEM_LIMIT)


def cost(flops, moved):
    return pl.CostEstimate(flops=flops, bytes_accessed=moved, transcendentals=0)


VMEM = pl.BlockSpec(memory_space=pltpu.VMEM)
SMEM = pl.BlockSpec(memory_space=pltpu.SMEM)


def panel_flip(array, flip):
    pairs = [(i, i ^ flip) for i in range(N_Y * N_X)]
    return lax.ppermute(array, "panel", pairs)


def beside(array, far):
    count = lax.axis_size("space")
    step = [1 if i % 2 == far else -1 for i in range(count)]
    pairs = [(i, i + by) for i, by in enumerate(step) if 0 <= i + by < count]
    return lax.ppermute(array, "space", pairs)


def call(kernel, outs, args, flops, name, scratch=(), specs=None):
    moved = sum(a.size * a.dtype.itemsize for a in args)
    return pl.pallas_call(
        kernel,
        in_specs=[VMEM] * len(args) if specs is None else specs,
        out_specs=[VMEM] * len(outs),
        out_shape=outs,
        scratch_shapes=scratch,
        compiler_params=params(),
        cost_estimate=cost(flops, moved),
        name=name,
    )(*args)


def join_kernel(*refs):
    out = refs[-1]
    at = 0
    for block in refs[:-1]:
        rows = block.shape[0]
        out[pl.ds(at, rows), :] = block[...]
        at += rows


def pack_kernel(by_y, other, *refs):
    half = other.shape[0]
    pair, stacked = refs[-2:]
    join_kernel(by_y, other, pair)
    join_kernel(*refs[:-2], stacked)


def pack_rhs_kernel(own, other, *refs):
    blocks, rhs = refs[:N_X], refs[N_X]
    pairs, stacked, keep, total = refs[N_X + 1 : 2 * N_X], *refs[-3:]
    half = blocks[0].shape[0]
    part = keep.shape[0]
    me = lax.axis_index("panel")
    y, x = me // N_X, me % N_X
    rows = pl.ds(pl.multiple_of(y * (N_X * part), N_X * part), N_X * part)
    both = rhs[rows, :].astype(F32) + other[pl.ds(half, N_X * part), :].astype(F32)
    total[...] = both.astype(BF)
    for d, pair in zip(ORDER[1:], pairs):
        pair[pl.ds(0, half), :] = own[pl.ds(0, half), :]
        pair[pl.ds(half, half), :] = other[pl.ds(0, half), :]
        at = pl.multiple_of((x + d) % N_X * part, part)
        pair[pl.ds(2 * half, part), :] = total[pl.ds(at, part), :]
    keep[...] = total[pl.ds(pl.multiple_of(x * part, part), part), :]
    join_kernel(*blocks, stacked)


def panel_along(array, dx):
    pairs = [(y * N_X + x, y * N_X + (x + dx) % N_X) for y in range(N_Y) for x in range(N_X)]
    return lax.ppermute(array, "panel", pairs)


def first_round(by_y, by_x):
    four = [by_x] + [panel_along(by_x, d) for d in ORDER[1:]]
    return by_y, panel_flip(by_y, N_X), *four


def pack(blocks):
    half, width = blocks[0].shape
    outs = [jax.ShapeDtypeStruct((n * half, width), BF) for n in (N_Y, N_X)]
    pair, stacked = call(pack_kernel, outs, blocks, half, "pack")
    return [pair] * N_X, stacked


def pack_rhs(blocks, rhs):
    half, width = blocks[2].shape
    part = rhs.shape[0] // (N_Y * N_X)
    shapes = [(2 * half + part, width)] * (N_X - 1) + [(N_X * half, width), (part, width)]
    *pairs, stacked, keep = call(
        pack_rhs_kernel, [jax.ShapeDtypeStruct(s, BF) for s in shapes], (*blocks, rhs), half, "pack",
        scratch=[pltpu.VMEM((N_X * part, width), BF)],
    )
    return [pairs[0], *pairs], stacked, keep


def second_round(pairs, stacked):
    moved = [pairs[0]] + [panel_along(pair, d) for pair, d in zip(pairs[1:], ORDER[1:])]
    return moved + [stacked, panel_flip(stacked, N_X)]


def piece_places(half):
    me = lax.axis_index("panel")
    y, x = me // N_X, me % N_X
    first = [(d, dy, 0) for d in ORDER for dy in range(N_Y)]
    second = [(d, dy, half) for dy in range(N_Y) for d in ORDER]
    return [
        ((y + dy) % N_Y * N_X + (x + N_X - d) % N_X) * (2 * half) + part
        for d, dy, part in first + second
    ]


def choose_kernel(n_pieces, wanted, matrix, *refs):
    pieces = refs[:n_pieces]
    near, far, acc, owned, owned32, chosen32 = refs[n_pieces:]
    half = pieces[-1].shape[0] // N_X
    sources = [(p, i * half) for p in pieces for i in range(p.shape[0] // half)]
    for (piece, start), at in zip(sources, piece_places(half)):
        rows = pl.ds(pl.multiple_of(at, half), half)
        block = piece[pl.ds(start, half), :]
        owned[rows, :] = block
        for i in range(2):
            at2 = pl.multiple_of(2 * at, 2 * half) + i
            owned32[pl.ds(at2, half, stride=2), :] = block[:, i * 128 : (i + 1) * 128].astype(F32)
    count = chosen32.shape[0] // 2
    group = 32

    def body(step, carry):
        first = pl.multiple_of(step * group, group)
        for j in range(group):
            row = pl.multiple_of(2 * wanted[first + j], 2)
            chosen32[pl.ds(2 * first + 2 * j, 2), :] = owned32[pl.ds(row, 2), :]
        return carry

    lax.fori_loop(0, count // group, body, 0)
    for i in range(2):
        lanes = pl.ds(i * 128, 128)
        near[:, lanes] = chosen32[pl.ds(i, count // 2, stride=2), :].astype(BF)
        far[:, lanes] = chosen32[pl.ds(count + i, count // 2, stride=2), :].astype(BF)
    depth = owned.shape[0]
    acc[...] = jnp.dot(matrix[:, pl.ds(0, depth)], owned[...], preferred_element_type=F32)


def choose(wanted, pieces, matrix):
    count = wanted.shape[0]
    width = pieces[0].shape[1]
    rows = 4 * pieces[-1].shape[0]
    half = jax.ShapeDtypeStruct((count // 2, width), BF)
    return call(
        functools.partial(choose_kernel, len(pieces)),
        [half, half, jax.ShapeDtypeStruct((matrix.shape[0], width), F32)],
        (wanted, matrix, *pieces),
        2 * rows * width * matrix.shape[0],
        "choose",
        scratch=[
            pltpu.VMEM((rows, width), BF),
            pltpu.VMEM((2 * rows, width // 2), F32),
            pltpu.VMEM((2 * count, width // 2), F32),
        ],
        specs=[SMEM] + [VMEM] * (1 + len(pieces)),
    )


def sum_kernel(keep, *refs):
    out = refs[-1]
    size = out.shape[0]
    total = keep[...].astype(F32)
    for moved in refs[:-1]:
        total = total + moved[pl.ds(moved.shape[0] - size, size), :].astype(F32)
    out[...] = total.astype(BF)


def transposed_dot(a, b):
    return lax.dot_general(a, b, (((0,), (0,)), ((), ())), preferred_element_type=F32)


def cut(rounded, by_y, by_x):
    half = by_x.shape[0]
    by_y[pl.ds(0, half), :] = rounded[:half]
    by_x[...] = rounded[half:]


def cut_with_rhs(rounded, basis, by_y, by_x, rhs):
    cut(rounded, by_y, by_x)
    rhs[...] = transposed_dot(basis[...], rounded).astype(BF)
    part = rhs.shape[0] // N_Y
    other = 1 - lax.axis_index("panel") // N_X
    by_y[pl.ds(by_x.shape[0], part), :] = rhs[pl.ds(pl.multiple_of(other * part, part), part), :]


def split_kernel(fields, basis, by_y, by_x, rhs):
    cut_with_rhs(fields[...].astype(BF), basis, by_y, by_x, rhs)


def margin_terms(matrix, acc, near, far):
    margin = near.shape[0]
    first = matrix.shape[1] - 2 * margin
    odd = lax.axis_index("space") % N_CORE
    near_at = pl.multiple_of(first + (1 - odd) * margin, margin)
    far_at = pl.multiple_of(first + odd * margin, margin)
    return (
        acc[...]
        + jnp.dot(matrix[:, pl.ds(near_at, margin)], near[...], preferred_element_type=F32)
        + jnp.dot(matrix[:, pl.ds(far_at, margin)], far[...], preferred_element_type=F32)
    )


def local_kernel(has_base, matrix, acc, near, far, basis, values, *refs):
    out, by_y, by_x = refs[-3:]
    total = margin_terms(matrix, acc, near, far)
    total = total + jnp.dot(basis[...], values[...], preferred_element_type=F32)
    if has_base:
        total = total + refs[0][...]
    out[...] = total
    cut(total.astype(BF), by_y, by_x)


def middle_kernel(matrix, acc, near, far, fields, basis, by_y, by_x, rhs):
    product = margin_terms(matrix, acc, near, far)
    cut_with_rhs((fields[...] - product).astype(BF), basis, by_y, by_x, rhs)


def residual_kernel(matrix, acc, near, far, fields, out):
    out[...] = fields[...] - margin_terms(matrix, acc, near, far)


def with_margins(kernel, outs, acc, matrix, near, far, extra, name):
    flops = 4 * acc.size * near.shape[0]
    return call(kernel, outs, (matrix, acc, near, far, *extra), flops, name)


def coarse_kernel(place, mine, other, matrix, out, kept):
    part = 32
    count = mine.shape[0] // part // 2
    for i, line in enumerate((mine, other)):
        core = lax.rem(place[0] + i, N_CORE)
        for k in range(2 * count):
            even = lax.rem(place[1] + count - k // 4 * 2, count)
            z = even + k % 2 * (1 - 2 * lax.rem(even, 2))
            y = lax.rem(place[2] + k // 2 % 2, 2)
            at = ((y * count + z) * N_CORE + core) * part
            kept[pl.ds(pl.multiple_of(at, part), part), :] = line[pl.ds(k * part, part), :]
    out[...] = jnp.dot(matrix[...], kept[...], preferred_element_type=F32).astype(BF)


def coarse_product(place, mine, other, matrix):
    rows, depth = matrix.shape
    width = mine.shape[1]
    args = (place, mine, other, matrix)
    return call(
        coarse_kernel,
        [jax.ShapeDtypeStruct((rows, width), BF)],
        args,
        2 * rows * depth * width,
        "coarse_product",
        scratch=[pltpu.VMEM((depth, width), BF)],
        specs=[SMEM] + [VMEM] * (len(args) - 1),
    )[0]


def on_device(
    fields, inverse_blocks, kernel_blocks, block_pattern, margin_rows, coarse_basis, coarse_inverse
):
    n_panel = lax.axis_size("panel")
    row_count, field_count = fields.shape
    land_sub = coarse_basis.shape[1]
    tiles_down = block_pattern.shape[1]
    tiles_across = block_pattern.shape[2]
    tile_edge = row_count // tiles_down
    pattern = block_pattern[0].astype(BF)
    masked_kernel = (
        kernel_blocks.reshape(tiles_down, tile_edge, tiles_across, tile_edge)
        * pattern[:, None, :, None]
    ).reshape(row_count, tiles_across * tile_edge)

    even = lax.axis_index("space") % N_CORE == 0
    from_near = jnp.where(even, margin_rows[0, 1], margin_rows[0, 0])
    from_far = jnp.where(even, margin_rows[0, 0], margin_rows[0, 1])
    wanted = jnp.concatenate([beside(from_near, 0), beside(from_far, 1)])
    n_space = lax.axis_size("space")
    line = n_space // N_CORE // 2
    space = lax.axis_index("space")
    place = jnp.stack([space % N_CORE, space // N_CORE % line, space // N_CORE // line])

    piece = jax.ShapeDtypeStruct((row_count // 2, field_count), BF)
    rhs_out = jax.ShapeDtypeStruct((land_sub, field_count), BF)
    first_piece = jax.ShapeDtypeStruct((row_count // 2 + land_sub // N_Y, field_count), BF)
    part_out = jax.ShapeDtypeStruct((land_sub // n_panel, field_count), BF)
    whole_out = jax.ShapeDtypeStruct((row_count, field_count), F32)

    def space_move(array, move):
        pairs = []
        for i in range(n_space):
            y, z, c = move(i // N_CORE // line, i // N_CORE % line, i % N_CORE)
            pairs.append((i, (y * line + z) * N_CORE + c))
        return lax.ppermute(array, "space", pairs)

    def joined(blocks):
        rows, width = blocks[0].shape
        out = jax.ShapeDtypeStruct((rows * len(blocks), width), BF)
        return call(join_kernel, [out], blocks, rows, "join")[0]

    def local_terms(first, by_x, rhs):
        four = [by_x] + [panel_along(by_x, d) for d in ORDER[1:]]
        pairs, stacked, keep = pack_rhs((first, panel_flip(first, N_X), *four), rhs)
        pieces = second_round(pairs, stacked)
        part = call(sum_kernel, [part_out], (keep, *pieces[1:N_X]), keep.size, "summed")[0]
        near, far, acc = choose(wanted, pieces, inverse_blocks)
        part, near, far = lax.optimization_barrier((part, near, far))
        far = beside(far, 1)
        flips = [lambda y, z, c, dz=dz, dy=dy: (y ^ dy, z ^ dz, c) for dz, dy in ((1, 0), (0, 1), (1, 1))]
        moved = [space_move(part, flip) for flip in flips]
        near = beside(near, 0)
        near, far, *moved = lax.optimization_barrier((near, far, *moved))
        four = joined([part, *moved])
        shifts = [lambda y, z, c, d=d: (y, (z + d) % line, c) for d in range(2, line, 2)]
        mine = joined([four] + [space_move(four, shift) for shift in shifts])
        other = space_move(mine, lambda y, z, c: (y, z, c ^ 1))
        total = coarse_product(place, mine, other, coarse_inverse)
        for flip in (N_X, 1, 2):
            total = (total.astype(F32) + panel_flip(total, flip).astype(F32)).astype(BF)
        return total, (acc, inverse_blocks, near, far)

    def kernel_terms(by_y, by_x):
        pieces = second_round(*pack(first_round(by_y, by_x)))
        near, far, acc = choose(wanted, pieces, masked_kernel)
        far, near = beside(far, 1), beside(near, 0)
        return acc, masked_kernel, near, far

    by_y, by_x, rhs = call(
        split_kernel, [first_piece, piece, rhs_out], (fields, coarse_basis),
        2 * fields.size * land_sub, "split",
    )
    base = None
    for step in range(2):
        values, terms = local_terms(by_y, by_x, rhs)
        extra = (coarse_basis, values) if base is None else (coarse_basis, values, base)
        base, by_y, by_x = with_margins(
            functools.partial(local_kernel, base is not None),
            [whole_out, piece, piece],
            *terms, extra, "local",
        )
        terms = kernel_terms(by_y, by_x)
        if step == 0:
            by_y, by_x, rhs = with_margins(
                middle_kernel, [first_piece, piece, rhs_out], *terms, (fields, coarse_basis), "middle"
            )
    (residual,) = with_margins(
        residual_kernel, [whole_out], *terms, (fields,), "residual"
    )
    return (base, residual)


def solution(mesh):
    in_specs = (
        P(("space", "panel"), None),
        P(("space", "panel"), None),
        P(("space", "panel"), None),
        P("space", "panel", None),
        P("space", None, None),
        P(("space", "panel"), None),
        P("space", "panel"),
    )
    out_specs = (P(("space", "panel"), None), P(("space", "panel"), None))
    return jax.shard_map(
        on_device, mesh=mesh, in_specs=in_specs, out_specs=out_specs, check_vma=False
    )
```

```python
import functools

import jax
import jax.numpy as jnp
from jax import lax
from jax.experimental import pallas as pl
from jax.experimental.pallas import tpu as pltpu
from jax.sharding import PartitionSpec as P

BF = jnp.bfloat16
F32 = jnp.float32
N_Y, N_X, N_CORE = 2, 4, 2
ORDER = (0, 1, 3, 2)
VMEM_LIMIT = 14 * 2**20


def params():
    return pltpu.CompilerParams(vmem_limit_bytes=VMEM_LIMIT)


def cost(flops, moved):
    return pl.CostEstimate(flops=flops, bytes_accessed=moved, transcendentals=0)


VMEM = pl.BlockSpec(memory_space=pltpu.VMEM)
SMEM = pl.BlockSpec(memory_space=pltpu.SMEM)


def panel_flip(array, flip):
    pairs = [(i, i ^ flip) for i in range(N_Y * N_X)]
    return lax.ppermute(array, "panel", pairs)


def beside(array, far):
    count = lax.axis_size("space")
    step = [1 if i % 2 == far else -1 for i in range(count)]
    pairs = [(i, i + by) for i, by in enumerate(step) if 0 <= i + by < count]
    return lax.ppermute(array, "space", pairs)


def call(kernel, outs, args, flops, name, scratch=(), specs=None):
    moved = sum(a.size * a.dtype.itemsize for a in args)
    return pl.pallas_call(
        kernel,
        in_specs=[VMEM] * len(args) if specs is None else specs,
        out_specs=[VMEM] * len(outs),
        out_shape=outs,
        scratch_shapes=scratch,
        compiler_params=params(),
        cost_estimate=cost(flops, moved),
        name=name,
    )(*args)


def join_kernel(*refs):
    out = refs[-1]
    at = 0
    for block in refs[:-1]:
        rows = block.shape[0]
        out[pl.ds(at, rows), :] = block[...]
        at += rows


def pack_kernel(by_y, other, *refs):
    half = other.shape[0]
    pair, stacked = refs[-2:]
    join_kernel(by_y, other, pair)
    join_kernel(*refs[:-2], stacked)


def pack_rhs_kernel(own, other, *refs):
    blocks, rhs = refs[:N_X], refs[N_X]
    pairs, stacked, keep, total = refs[N_X + 1 : 2 * N_X], *refs[-3:]
    half = blocks[0].shape[0]
    part = keep.shape[0]
    me = lax.axis_index("panel")
    y, x = me // N_X, me % N_X
    rows = pl.ds(pl.multiple_of(y * (N_X * part), N_X * part), N_X * part)
    both = rhs[rows, :].astype(F32) + other[pl.ds(half, N_X * part), :].astype(F32)
    total[...] = both.astype(BF)
    for d, pair in zip(ORDER[1:], pairs):
        pair[pl.ds(0, half), :] = own[pl.ds(0, half), :]
        pair[pl.ds(half, half), :] = other[pl.ds(0, half), :]
        at = pl.multiple_of((x + d) % N_X * part, part)
        pair[pl.ds(2 * half, part), :] = total[pl.ds(at, part), :]
    keep[...] = total[pl.ds(pl.multiple_of(x * part, part), part), :]
    join_kernel(*blocks, stacked)


def panel_along(array, dx):
    pairs = [(y * N_X + x, y * N_X + (x + dx) % N_X) for y in range(N_Y) for x in range(N_X)]
    return lax.ppermute(array, "panel", pairs)


def first_round(by_y, by_x):
    four = [by_x] + [panel_along(by_x, d) for d in ORDER[1:]]
    return by_y, panel_flip(by_y, N_X), *four


def pack(blocks):
    half, width = blocks[0].shape
    outs = [jax.ShapeDtypeStruct((n * half, width), BF) for n in (N_Y, N_X)]
    pair, stacked = call(pack_kernel, outs, blocks, half, "pack")
    return [pair] * N_X, stacked


def pack_rhs(blocks, rhs):
    half, width = blocks[2].shape
    part = rhs.shape[0] // (N_Y * N_X)
    shapes = [(2 * half + part, width)] * (N_X - 1) + [(N_X * half, width), (part, width)]
    *pairs, stacked, keep = call(
        pack_rhs_kernel, [jax.ShapeDtypeStruct(s, BF) for s in shapes], (*blocks, rhs), half, "pack",
        scratch=[pltpu.VMEM((N_X * part, width), BF)],
    )
    return [pairs[0], *pairs], stacked, keep


def second_round(pairs, stacked):
    moved = [pairs[0]] + [panel_along(pair, d) for pair, d in zip(pairs[1:], ORDER[1:])]
    return moved + [stacked, panel_flip(stacked, N_X)]


def piece_places(half):
    me = lax.axis_index("panel")
    y, x = me // N_X, me % N_X
    first = [(d, dy, 0) for d in ORDER for dy in range(N_Y)]
    second = [(d, dy, half) for dy in range(N_Y) for d in ORDER]
    return [
        ((y + dy) % N_Y * N_X + (x + N_X - d) % N_X) * (2 * half) + part
        for d, dy, part in first + second
    ]


def choose_kernel(n_pieces, wanted, matrix, *refs):
    pieces = refs[:n_pieces]
    near, far, acc, owned, owned32, chosen32 = refs[n_pieces:]
    half = pieces[-1].shape[0] // N_X
    sources = [(p, i * half) for p in pieces for i in range(p.shape[0] // half)]
    for (piece, start), at in zip(sources, piece_places(half)):
        rows = pl.ds(pl.multiple_of(at, half), half)
        block = piece[pl.ds(start, half), :]
        owned[rows, :] = block
        for i in range(2):
            at2 = pl.multiple_of(2 * at, 2 * half) + i
            owned32[pl.ds(at2, half, stride=2), :] = block[:, i * 128 : (i + 1) * 128].astype(F32)
    count = chosen32.shape[0] // 2
    group = 32

    def body(step, carry):
        first = pl.multiple_of(step * group, group)
        for j in range(group):
            row = pl.multiple_of(2 * wanted[first + j], 2)
            chosen32[pl.ds(2 * first + 2 * j, 2), :] = owned32[pl.ds(row, 2), :]
        return carry

    lax.fori_loop(0, count // group, body, 0)
    for i in range(2):
        lanes = pl.ds(i * 128, 128)
        near[:, lanes] = chosen32[pl.ds(i, count // 2, stride=2), :].astype(BF)
        far[:, lanes] = chosen32[pl.ds(count + i, count // 2, stride=2), :].astype(BF)
    depth = owned.shape[0]
    acc[...] = jnp.dot(matrix[:, pl.ds(0, depth)], owned[...], preferred_element_type=F32)


def choose(wanted, pieces, matrix):
    count = wanted.shape[0]
    width = pieces[0].shape[1]
    rows = 4 * pieces[-1].shape[0]
    half = jax.ShapeDtypeStruct((count // 2, width), BF)
    return call(
        functools.partial(choose_kernel, len(pieces)),
        [half, half, jax.ShapeDtypeStruct((matrix.shape[0], width), F32)],
        (wanted, matrix, *pieces),
        2 * rows * width * matrix.shape[0],
        "choose",
        scratch=[
            pltpu.VMEM((rows, width), BF),
            pltpu.VMEM((2 * rows, width // 2), F32),
            pltpu.VMEM((2 * count, width // 2), F32),
        ],
        specs=[SMEM] + [VMEM] * (1 + len(pieces)),
    )


def sum_kernel(keep, *refs):
    out = refs[-1]
    size = out.shape[0]
    total = keep[...].astype(F32)
    for moved in refs[:-1]:
        total = total + moved[pl.ds(moved.shape[0] - size, size), :].astype(F32)
    out[...] = total.astype(BF)


def hold_kernel(source, out, arrived):
    copy = pltpu.make_async_copy(source, out, arrived)
    copy.start()
    copy.wait()


def hold(array):
    return call(
        hold_kernel, [jax.ShapeDtypeStruct(array.shape, array.dtype)], (array,), 0, "hold",
        scratch=[pltpu.SemaphoreType.DMA], specs=[pl.BlockSpec(memory_space=pl.ANY)],
    )[0]


def transposed_dot(a, b):
    return lax.dot_general(a, b, (((0,), (0,)), ((), ())), preferred_element_type=F32)


def cut(rounded, by_y, by_x):
    half = by_x.shape[0]
    by_y[pl.ds(0, half), :] = rounded[:half]
    by_x[...] = rounded[half:]


def cut_with_rhs(rounded, basis, by_y, by_x, rhs):
    cut(rounded, by_y, by_x)
    rhs[...] = transposed_dot(basis[...], rounded).astype(BF)
    part = rhs.shape[0] // N_Y
    other = 1 - lax.axis_index("panel") // N_X
    by_y[pl.ds(by_x.shape[0], part), :] = rhs[pl.ds(pl.multiple_of(other * part, part), part), :]


def split_kernel(fields, basis, by_y, by_x, rhs):
    cut_with_rhs(fields[...].astype(BF), basis, by_y, by_x, rhs)


def margin_terms(matrix, acc, near, far):
    margin = near.shape[0]
    first = matrix.shape[1] - 2 * margin
    odd = lax.axis_index("space") % N_CORE
    near_at = pl.multiple_of(first + (1 - odd) * margin, margin)
    far_at = pl.multiple_of(first + odd * margin, margin)
    return (
        acc[...]
        + jnp.dot(matrix[:, pl.ds(near_at, margin)], near[...], preferred_element_type=F32)
        + jnp.dot(matrix[:, pl.ds(far_at, margin)], far[...], preferred_element_type=F32)
    )


def margin_kernel(matrix, acc, near, far, out):
    out[...] = margin_terms(matrix, acc, near, far)


def local_kernel(has_base, acc, basis, values, *refs):
    out, by_y, by_x = refs[-3:]
    total = acc[...] + jnp.dot(basis[...], values[...], preferred_element_type=F32)
    if has_base:
        total = total + refs[0][...]
    out[...] = total
    cut(total.astype(BF), by_y, by_x)


def middle_kernel(matrix, acc, near, far, fields, basis, by_y, by_x, rhs):
    product = margin_terms(matrix, acc, near, far)
    cut_with_rhs((fields[...] - product).astype(BF), basis, by_y, by_x, rhs)


def residual_kernel(matrix, acc, near, far, fields, out):
    out[...] = fields[...] - margin_terms(matrix, acc, near, far)


def with_margins(kernel, outs, acc, matrix, near, far, extra, name):
    flops = 4 * acc.size * near.shape[0]
    return call(kernel, outs, (matrix, acc, near, far, *extra), flops, name)


def coarse_kernel(place, mine, other, matrix, out, kept):
    part = 32
    count = mine.shape[0] // part // 2
    for i, line in enumerate((mine, other)):
        core = lax.rem(place[0] + i, N_CORE)
        for k in range(2 * count):
            even = lax.rem(place[1] + count - k // 4 * 2, count)
            z = even + k % 2 * (1 - 2 * lax.rem(even, 2))
            y = lax.rem(place[2] + k // 2 % 2, 2)
            at = ((y * count + z) * N_CORE + core) * part
            kept[pl.ds(pl.multiple_of(at, part), part), :] = line[pl.ds(k * part, part), :]
    out[...] = jnp.dot(matrix[...], kept[...], preferred_element_type=F32).astype(BF)


def coarse_product(place, mine, other, matrix):
    rows, depth = matrix.shape
    width = mine.shape[1]
    args = (place, mine, other, matrix)
    return call(
        coarse_kernel,
        [jax.ShapeDtypeStruct((rows, width), BF)],
        args,
        2 * rows * depth * width,
        "coarse_product",
        scratch=[pltpu.VMEM((depth, width), BF)],
        specs=[SMEM] + [VMEM] * (len(args) - 1),
    )[0]


def on_device(
    fields, inverse_blocks, kernel_blocks, block_pattern, margin_rows, coarse_basis, coarse_inverse
):
    n_panel = lax.axis_size("panel")
    row_count, field_count = fields.shape
    land_sub = coarse_basis.shape[1]
    tiles_down = block_pattern.shape[1]
    tiles_across = block_pattern.shape[2]
    tile_edge = row_count // tiles_down
    pattern = block_pattern[0].astype(BF)
    masked_kernel = (
        kernel_blocks.reshape(tiles_down, tile_edge, tiles_across, tile_edge)
        * pattern[:, None, :, None]
    ).reshape(row_count, tiles_across * tile_edge)

    inverse_blocks = hold(inverse_blocks)
    even = lax.axis_index("space") % N_CORE == 0
    from_near = jnp.where(even, margin_rows[0, 1], margin_rows[0, 0])
    from_far = jnp.where(even, margin_rows[0, 0], margin_rows[0, 1])
    n_space = lax.axis_size("space")
    line = n_space // N_CORE // 2
    space = lax.axis_index("space")
    place = jnp.stack([space % N_CORE, space // N_CORE % line, space // N_CORE // line])

    piece = jax.ShapeDtypeStruct((row_count // 2, field_count), BF)
    rhs_out = jax.ShapeDtypeStruct((land_sub, field_count), BF)
    first_piece = jax.ShapeDtypeStruct((row_count // 2 + land_sub // N_Y, field_count), BF)
    part_out = jax.ShapeDtypeStruct((land_sub // n_panel, field_count), BF)
    whole_out = jax.ShapeDtypeStruct((row_count, field_count), F32)

    def space_move(array, move):
        pairs = []
        for i in range(n_space):
            y, z, c = move(i // N_CORE // line, i // N_CORE % line, i % N_CORE)
            pairs.append((i, (y * line + z) * N_CORE + c))
        return lax.ppermute(array, "space", pairs)

    def joined(blocks):
        rows, width = blocks[0].shape
        out = jax.ShapeDtypeStruct((rows * len(blocks), width), BF)
        return call(join_kernel, [out], blocks, rows, "join")[0]

    def local_terms(first, by_x, rhs, wanted):
        four = [by_x] + [panel_along(by_x, d) for d in ORDER[1:]]
        if wanted is None:
            mine, four[1] = lax.optimization_barrier((from_near, four[1]))
            wanted_near = beside(mine, 0)
        pairs, stacked, keep = pack_rhs((first, panel_flip(first, N_X), *four), rhs)
        pieces = second_round(pairs, stacked)
        if wanted is None:
            mine, pieces[1] = lax.optimization_barrier((from_far, pieces[1]))
            wanted = jnp.concatenate([wanted_near, beside(mine, 1)])
        part = call(sum_kernel, [part_out], (keep, *pieces[1:N_X]), keep.size, "summed")[0]
        near, far, acc = choose(wanted, pieces, inverse_blocks)
        part, near, far = lax.optimization_barrier((part, near, far))
        far = beside(far, 1)
        flips = [lambda y, z, c, dz=dz, dy=dy: (y ^ dy, z ^ dz, c) for dz, dy in ((1, 0), (0, 1), (1, 1))]
        moved = [space_move(part, flip) for flip in flips]
        near = beside(near, 0)
        (acc,) = with_margins(
            margin_kernel, [whole_out], acc, inverse_blocks, near, far, (), "margins"
        )
        acc, *moved = lax.optimization_barrier((acc, *moved))
        four = joined([part, *moved])
        shifts = [lambda y, z, c, d=d: (y, (z + d) % line, c) for d in range(2, line, 2)]
        mine = joined([four] + [space_move(four, shift) for shift in shifts])
        other = space_move(mine, lambda y, z, c: (y, z, c ^ 1))
        total = coarse_product(place, mine, other, coarse_inverse)
        total = (total.astype(F32) + panel_flip(total, N_X).astype(F32)).astype(BF)
        others = [panel_along(total, d).astype(F32) for d in (2, 1, 3)]
        total = (total.astype(F32) + others[0] + others[1] + others[2]).astype(BF)
        return total, acc, wanted

    def kernel_terms(by_y, by_x, wanted):
        pieces = second_round(*pack(first_round(by_y, by_x)))
        near, far, acc = choose(wanted, pieces, masked_kernel)
        far, near = beside(far, 1), beside(near, 0)
        return acc, masked_kernel, near, far

    by_y, by_x, rhs = call(
        split_kernel, [first_piece, piece, rhs_out], (fields, coarse_basis),
        2 * fields.size * land_sub, "split",
    )
    base = wanted = None
    for step in range(2):
        values, terms, wanted = local_terms(by_y, by_x, rhs, wanted)
        extra = (coarse_basis, values) if base is None else (coarse_basis, values, base)
        base, by_y, by_x = call(
            functools.partial(local_kernel, base is not None),
            [whole_out, piece, piece], (terms, *extra), 2 * fields.size * land_sub, "local",
        )
        terms = kernel_terms(by_y, by_x, wanted)
        if step == 0:
            by_y, by_x, rhs = with_margins(
                middle_kernel, [first_piece, piece, rhs_out], *terms, (fields, coarse_basis), "middle"
            )
    (residual,) = with_margins(
        residual_kernel, [whole_out], *terms, (fields,), "residual"
    )
    return (base, residual)


def solution(mesh):
    in_specs = (
        P(("space", "panel"), None),
        P(("space", "panel"), None),
        P(("space", "panel"), None),
        P("space", "panel", None),
        P("space", None, None),
        P(("space", "panel"), None),
        P("space", "panel"),
    )
    out_specs = (P(("space", "panel"), None), P(("space", "panel"), None))
    return jax.shard_map(
        on_device, mesh=mesh, in_specs=in_specs, out_specs=out_specs, check_vma=False
    )
```

```python
import functools

import jax
import jax.numpy as jnp
from jax import lax
from jax.experimental import pallas as pl
from jax.experimental.pallas import tpu as pltpu
from jax.sharding import PartitionSpec as P

BF = jnp.bfloat16
F32 = jnp.float32
N_Y, N_X, N_CORE = 2, 4, 2
ORDER = (0, 1, 3, 2)
VMEM_LIMIT = 14 * 2**20


def params():
    return pltpu.CompilerParams(vmem_limit_bytes=VMEM_LIMIT)


def cost(flops, moved):
    return pl.CostEstimate(flops=flops, bytes_accessed=moved, transcendentals=0)


VMEM = pl.BlockSpec(memory_space=pltpu.VMEM)
SMEM = pl.BlockSpec(memory_space=pltpu.SMEM)


def panel_flip(array, flip):
    pairs = [(i, i ^ flip) for i in range(N_Y * N_X)]
    return lax.ppermute(array, "panel", pairs)


def beside(array, far):
    count = lax.axis_size("space")
    step = [1 if i % 2 == far else -1 for i in range(count)]
    pairs = [(i, i + by) for i, by in enumerate(step) if 0 <= i + by < count]
    return lax.ppermute(array, "space", pairs)


def call(kernel, outs, args, flops, name, scratch=(), specs=None):
    moved = sum(a.size * a.dtype.itemsize for a in args)
    return pl.pallas_call(
        kernel,
        in_specs=[VMEM] * len(args) if specs is None else specs,
        out_specs=[VMEM] * len(outs),
        out_shape=outs,
        scratch_shapes=scratch,
        compiler_params=params(),
        cost_estimate=cost(flops, moved),
        name=name,
    )(*args)


def join_kernel(*refs):
    out = refs[-1]
    at = 0
    for block in refs[:-1]:
        rows = block.shape[0]
        out[pl.ds(at, rows), :] = block[...]
        at += rows


def pack_kernel(by_y, other, *refs):
    half = other.shape[0]
    pair, stacked = refs[-2:]
    join_kernel(by_y, other, pair)
    join_kernel(*refs[:-2], stacked)


def pack_rhs_kernel(own, other, *refs):
    blocks, rhs = refs[:N_X], refs[N_X]
    pairs, stacked, keep, total = refs[N_X + 1 : 2 * N_X], *refs[-3:]
    half = blocks[0].shape[0]
    part = keep.shape[0]
    me = lax.axis_index("panel")
    y, x = me // N_X, me % N_X
    rows = pl.ds(pl.multiple_of(y * (N_X * part), N_X * part), N_X * part)
    both = rhs[rows, :].astype(F32) + other[pl.ds(half, N_X * part), :].astype(F32)
    total[...] = both.astype(BF)
    for d, pair in zip(ORDER[1:], pairs):
        pair[pl.ds(0, half), :] = own[pl.ds(0, half), :]
        pair[pl.ds(half, half), :] = other[pl.ds(0, half), :]
        at = pl.multiple_of((x + d) % N_X * part, part)
        pair[pl.ds(2 * half, part), :] = total[pl.ds(at, part), :]
    keep[...] = total[pl.ds(pl.multiple_of(x * part, part), part), :]
    join_kernel(*blocks, stacked)


def panel_along(array, dx):
    pairs = [(y * N_X + x, y * N_X + (x + dx) % N_X) for y in range(N_Y) for x in range(N_X)]
    return lax.ppermute(array, "panel", pairs)


def first_round(by_y, by_x):
    four = [by_x] + [panel_along(by_x, d) for d in ORDER[1:]]
    return by_y, panel_flip(by_y, N_X), *four


def pack(blocks):
    half, width = blocks[0].shape
    outs = [jax.ShapeDtypeStruct((n * half, width), BF) for n in (N_Y, N_X)]
    pair, stacked = call(pack_kernel, outs, blocks, half, "pack")
    return [pair] * N_X, stacked


def pack_rhs(blocks, rhs):
    half, width = blocks[2].shape
    part = rhs.shape[0] // (N_Y * N_X)
    shapes = [(2 * half + part, width)] * (N_X - 1) + [(N_X * half, width), (part, width)]
    *pairs, stacked, keep = call(
        pack_rhs_kernel, [jax.ShapeDtypeStruct(s, BF) for s in shapes], (*blocks, rhs), half, "pack",
        scratch=[pltpu.VMEM((N_X * part, width), BF)],
    )
    return [pairs[0], *pairs], stacked, keep


def second_round(pairs, stacked):
    moved = [pairs[0]] + [panel_along(pair, d) for pair, d in zip(pairs[1:], ORDER[1:])]
    return moved + [stacked, panel_flip(stacked, N_X)]


def piece_places(half):
    me = lax.axis_index("panel")
    y, x = me // N_X, me % N_X
    first = [(d, dy, 0) for d in ORDER for dy in range(N_Y)]
    second = [(d, dy, half) for dy in range(N_Y) for d in ORDER]
    return [
        ((y + dy) % N_Y * N_X + (x + N_X - d) % N_X) * (2 * half) + part
        for d, dy, part in first + second
    ]


def choose_kernel(n_pieces, wanted, matrix, *refs):
    pieces = refs[:n_pieces]
    near, far, acc, owned, owned32, chosen32 = refs[n_pieces:]
    half = pieces[-1].shape[0] // N_X
    sources = [(p, i * half) for p in pieces for i in range(p.shape[0] // half)]
    for (piece, start), at in zip(sources, piece_places(half)):
        rows = pl.ds(pl.multiple_of(at, half), half)
        block = piece[pl.ds(start, half), :]
        owned[rows, :] = block
        for i in range(2):
            at2 = pl.multiple_of(2 * at, 2 * half) + i
            owned32[pl.ds(at2, half, stride=2), :] = block[:, i * 128 : (i + 1) * 128].astype(F32)
    count = chosen32.shape[0] // 2
    group = 32

    def body(step, carry):
        first = pl.multiple_of(step * group, group)
        for j in range(group):
            row = pl.multiple_of(2 * wanted[first + j], 2)
            chosen32[pl.ds(2 * first + 2 * j, 2), :] = owned32[pl.ds(row, 2), :]
        return carry

    lax.fori_loop(0, count // group, body, 0)
    for i in range(2):
        lanes = pl.ds(i * 128, 128)
        near[:, lanes] = chosen32[pl.ds(i, count // 2, stride=2), :].astype(BF)
        far[:, lanes] = chosen32[pl.ds(count + i, count // 2, stride=2), :].astype(BF)
    depth = owned.shape[0]
    acc[...] = jnp.dot(matrix[:, pl.ds(0, depth)], owned[...], preferred_element_type=F32)


def choose(wanted, pieces, matrix):
    count = wanted.shape[0]
    width = pieces[0].shape[1]
    rows = 4 * pieces[-1].shape[0]
    half = jax.ShapeDtypeStruct((count // 2, width), BF)
    return call(
        functools.partial(choose_kernel, len(pieces)),
        [half, half, jax.ShapeDtypeStruct((matrix.shape[0], width), F32)],
        (wanted, matrix, *pieces),
        2 * rows * width * matrix.shape[0],
        "choose",
        scratch=[
            pltpu.VMEM((rows, width), BF),
            pltpu.VMEM((2 * rows, width // 2), F32),
            pltpu.VMEM((2 * count, width // 2), F32),
        ],
        specs=[SMEM] + [VMEM] * (1 + len(pieces)),
    )


def sum_kernel(keep, *refs):
    out = refs[-1]
    size = out.shape[0]
    total = keep[...].astype(F32)
    for moved in refs[:-1]:
        total = total + moved[pl.ds(moved.shape[0] - size, size), :].astype(F32)
    out[...] = total.astype(BF)


def hold_kernel(source, out, arrived):
    copy = pltpu.make_async_copy(source, out, arrived)
    copy.start()
    copy.wait()


def hold(array):
    return call(
        hold_kernel, [jax.ShapeDtypeStruct(array.shape, array.dtype)], (array,), 0, "hold",
        scratch=[pltpu.SemaphoreType.DMA], specs=[pl.BlockSpec(memory_space=pl.ANY)],
    )[0]


def transposed_dot(a, b):
    return lax.dot_general(a, b, (((0,), (0,)), ((), ())), preferred_element_type=F32)


def cut(rounded, by_y, by_x):
    half = by_x.shape[0]
    by_y[pl.ds(0, half), :] = rounded[:half]
    by_x[...] = rounded[half:]


def cut_with_rhs(rounded, basis, by_y, by_x, rhs):
    cut(rounded, by_y, by_x)
    rhs[...] = transposed_dot(basis[...], rounded).astype(BF)
    part = rhs.shape[0] // N_Y
    other = 1 - lax.axis_index("panel") // N_X
    by_y[pl.ds(by_x.shape[0], part), :] = rhs[pl.ds(pl.multiple_of(other * part, part), part), :]


def split_kernel(fields, basis, by_y, by_x, rhs):
    cut_with_rhs(fields[...].astype(BF), basis, by_y, by_x, rhs)


def margin_terms(matrix, acc, near, far):
    margin = near.shape[0]
    first = matrix.shape[1] - 2 * margin
    odd = lax.axis_index("space") % N_CORE
    near_at = pl.multiple_of(first + (1 - odd) * margin, margin)
    far_at = pl.multiple_of(first + odd * margin, margin)
    return (
        acc[...]
        + jnp.dot(matrix[:, pl.ds(near_at, margin)], near[...], preferred_element_type=F32)
        + jnp.dot(matrix[:, pl.ds(far_at, margin)], far[...], preferred_element_type=F32)
    )


def margin_kernel(matrix, acc, near, far, out):
    out[...] = margin_terms(matrix, acc, near, far)


def local_kernel(has_base, acc, basis, values, *refs):
    out, by_y, by_x = refs[-3:]
    total = acc[...] + jnp.dot(basis[...], values[...], preferred_element_type=F32)
    if has_base:
        total = total + refs[0][...]
    out[...] = total
    cut(total.astype(BF), by_y, by_x)


def middle_kernel(matrix, acc, near, far, fields, basis, by_y, by_x, rhs):
    product = margin_terms(matrix, acc, near, far)
    cut_with_rhs((fields[...] - product).astype(BF), basis, by_y, by_x, rhs)


def residual_kernel(matrix, acc, near, far, fields, out):
    out[...] = fields[...] - margin_terms(matrix, acc, near, far)


def with_margins(kernel, outs, acc, matrix, near, far, extra, name):
    flops = 4 * acc.size * near.shape[0]
    return call(kernel, outs, (matrix, acc, near, far, *extra), flops, name)


def coarse_kernel(place, mine, other, matrix, out, kept):
    part = 32
    count = mine.shape[0] // part // 2
    for i, line in enumerate((mine, other)):
        core = lax.rem(place[0] + i, N_CORE)
        for k in range(2 * count):
            from_z = place[1] + k // 4 % 2 * (1 - 2 * lax.rem(place[1], 2))
            z = lax.rem(from_z + count - k % 4 * 2, count)
            y = lax.rem(place[2] + k // 8, 2)
            at = ((y * count + z) * N_CORE + core) * part
            kept[pl.ds(pl.multiple_of(at, part), part), :] = line[pl.ds(k * part, part), :]
    out[...] = jnp.dot(matrix[...], kept[...], preferred_element_type=F32).astype(BF)


def coarse_product(place, mine, other, matrix):
    rows, depth = matrix.shape
    width = mine.shape[1]
    args = (place, mine, other, matrix)
    return call(
        coarse_kernel,
        [jax.ShapeDtypeStruct((rows, width), BF)],
        args,
        2 * rows * depth * width,
        "coarse_product",
        scratch=[pltpu.VMEM((depth, width), BF)],
        specs=[SMEM] + [VMEM] * (len(args) - 1),
    )[0]


def on_device(
    fields, inverse_blocks, kernel_blocks, block_pattern, margin_rows, coarse_basis, coarse_inverse
):
    n_panel = lax.axis_size("panel")
    row_count, field_count = fields.shape
    land_sub = coarse_basis.shape[1]
    tiles_down = block_pattern.shape[1]
    tiles_across = block_pattern.shape[2]
    tile_edge = row_count // tiles_down
    pattern = block_pattern[0].astype(BF)
    masked_kernel = (
        kernel_blocks.reshape(tiles_down, tile_edge, tiles_across, tile_edge)
        * pattern[:, None, :, None]
    ).reshape(row_count, tiles_across * tile_edge)

    inverse_blocks = hold(inverse_blocks)
    even = lax.axis_index("space") % N_CORE == 0
    from_near = jnp.where(even, margin_rows[0, 1], margin_rows[0, 0])
    from_far = jnp.where(even, margin_rows[0, 0], margin_rows[0, 1])
    n_space = lax.axis_size("space")
    line = n_space // N_CORE // 2
    space = lax.axis_index("space")
    place = jnp.stack([space % N_CORE, space // N_CORE % line, space // N_CORE // line])

    piece = jax.ShapeDtypeStruct((row_count // 2, field_count), BF)
    rhs_out = jax.ShapeDtypeStruct((land_sub, field_count), BF)
    first_piece = jax.ShapeDtypeStruct((row_count // 2 + land_sub // N_Y, field_count), BF)
    part_out = jax.ShapeDtypeStruct((land_sub // n_panel, field_count), BF)
    whole_out = jax.ShapeDtypeStruct((row_count, field_count), F32)

    def space_move(array, move):
        pairs = []
        for i in range(n_space):
            y, z, c = move(i // N_CORE // line, i // N_CORE % line, i % N_CORE)
            pairs.append((i, (y * line + z) * N_CORE + c))
        return lax.ppermute(array, "space", pairs)

    def joined(blocks):
        rows, width = blocks[0].shape
        out = jax.ShapeDtypeStruct((rows * len(blocks), width), BF)
        return call(join_kernel, [out], blocks, rows, "join")[0]

    def local_terms(first, by_x, rhs, wanted):
        four = [by_x] + [panel_along(by_x, d) for d in ORDER[1:]]
        if wanted is None:
            mine, four[1] = lax.optimization_barrier((from_near, four[1]))
            wanted_near = beside(mine, 0)
        pairs, stacked, keep = pack_rhs((first, panel_flip(first, N_X), *four), rhs)
        pieces = second_round(pairs, stacked)
        if wanted is None:
            mine, pieces[1] = lax.optimization_barrier((from_far, pieces[1]))
            wanted = jnp.concatenate([wanted_near, beside(mine, 1)])
        part = call(sum_kernel, [part_out], (keep, *pieces[1:N_X]), keep.size, "summed")[0]
        near, far, acc = choose(wanted, pieces, inverse_blocks)
        part, near, far = lax.optimization_barrier((part, near, far))
        far = beside(far, 1)
        shifts = [lambda y, z, c, d=d: (y, (z + d) % line, c) for d in range(2, line, 2)]
        moved = [space_move(part, shift) for shift in shifts]
        near = beside(near, 0)
        (acc,) = with_margins(
            margin_kernel, [whole_out], acc, inverse_blocks, near, far, (), "margins"
        )
        acc, *moved = lax.optimization_barrier((acc, *moved))
        four = joined([part, *moved])
        flips = [lambda y, z, c, dz=dz, dy=dy: (y ^ dy, z ^ dz, c) for dz, dy in ((1, 0), (0, 1), (1, 1))]
        mine = joined([four] + [space_move(four, flip) for flip in flips])
        other = space_move(mine, lambda y, z, c: (y, z, c ^ 1))
        total = coarse_product(place, mine, other, coarse_inverse)
        total = (total.astype(F32) + panel_flip(total, N_X).astype(F32)).astype(BF)
        others = [panel_along(total, d).astype(F32) for d in (2, 1, 3)]
        total = (total.astype(F32) + others[0] + others[1] + others[2]).astype(BF)
        return total, acc, wanted

    def kernel_terms(by_y, by_x, wanted):
        pieces = second_round(*pack(first_round(by_y, by_x)))
        near, far, acc = choose(wanted, pieces, masked_kernel)
        far, near = beside(far, 1), beside(near, 0)
        return acc, masked_kernel, near, far

    by_y, by_x, rhs = call(
        split_kernel, [first_piece, piece, rhs_out], (fields, coarse_basis),
        2 * fields.size * land_sub, "split",
    )
    base = wanted = None
    for step in range(2):
        values, terms, wanted = local_terms(by_y, by_x, rhs, wanted)
        extra = (coarse_basis, values) if base is None else (coarse_basis, values, base)
        base, by_y, by_x = call(
            functools.partial(local_kernel, base is not None),
            [whole_out, piece, piece], (terms, *extra), 2 * fields.size * land_sub, "local",
        )
        terms = kernel_terms(by_y, by_x, wanted)
        if step == 0:
            by_y, by_x, rhs = with_margins(
                middle_kernel, [first_piece, piece, rhs_out], *terms, (fields, coarse_basis), "middle"
            )
    (residual,) = with_margins(
        residual_kernel, [whole_out], *terms, (fields,), "residual"
    )
    return (base, residual)


def solution(mesh):
    in_specs = (
        P(("space", "panel"), None),
        P(("space", "panel"), None),
        P(("space", "panel"), None),
        P("space", "panel", None),
        P("space", None, None),
        P(("space", "panel"), None),
        P("space", "panel"),
    )
    out_specs = (P(("space", "panel"), None), P(("space", "panel"), None))
    return jax.shard_map(
        on_device, mesh=mesh, in_specs=in_specs, out_specs=out_specs, check_vma=False
    )
```
